32 devices in a mesh: groups: 2 (over y), dp: 4 (over x, core), tensor: 4 (over z).
Axes of the slice: x: 2, y: 2, z: 4, core: 2. Of those that a mesh axis runs over, the one named last changes fastest.
Arguments:
- tokens: bfloat16 [4096, 4096], P(('groups', 'dp')), parts along dimension 0, may hold values from -6 to 6
- weight: bfloat16 [4096, 14336], P(None, 'tensor'), may hold values from -0.09375 to 0.09375
- grad_act: bfloat16 [4096, 14336], P(('groups', 'dp'), 'tensor'), parts along dimension 0, may hold values from -6 to 6
- proj_in: bfloat16 [4096, 64], P('tensor'), may hold values from -0.09375 to 0.09375
- proj_out: bfloat16 [14336, 64], P('tensor'), may hold values from -0.046875 to 0.046875
- query_bank: float32 [128, 4096], P(('groups', 'dp')), parts along dimension 0, may hold values from -6 to 6
- query_index: int32 [256], P('groups'), parts along dimension 0, may hold values from 0 to 63, as said below
Outputs:
- grad_in_t: bfloat16 [4096, 4096], P('tensor', ('groups', 'dp')), parts along dimension 1
- gram: float32 [8192, 4096], P(('groups', 'dp', 'tensor')), parts along dimension 0
- scores: float32 [16, 128], P(('groups', 'dp')), parts along dimension 0
The draws below stay inside these ranges and needn't reach their ends.
There are 2 independent parts, one for each index of `groups`. The reference program is written for one: setup_inputs(seed, part) draws one part's arguments, and reference() takes and returns one part's arrays. A program takes and returns all parts, laid end to end along the dimension named above; an argument that names none is the same for every part. Nothing has to cross between parts.
Inputs may be any that keep to these rules, and one draw needn't show every extreme that they name: `query_index`: rows of query_bank to score, repeats allowed.
All inputs are finite; a program needn't handle non-finite values.
Results may differ from the reference program's by a relative error of at most 0.005.
Values sent between devices are 32-bit elements; how exact they have to be, the bound alone decides.
No kernel may reach another device: no remote copies, remote signals or barrier semaphores. Data moves between devices by JAX's collectives and lax.ppermute only.
A program may use at most 192 MiB of HBM per device.

```python
import math
import jax
import jax.numpy as jnp
from jax import lax

D = 4096
FF = 14336
K_IN = 64
K_OUT = 64
LEN = 256
NQ = 128
SK = 4096
DOCS = 8
TOKENS = 2048
QBANK = 64


def draw_query_index(key, part):
    key = jax.random.fold_in(key, 7)
    picks = jax.random.randint(key, (NQ,), 0, QBANK, dtype=jnp.int32)
    picks = picks.at[0].set(QBANK - 1)
    return picks.at[1].set(0)


def levels(stream_key, dims, pieces, smallest, top_value):
    gain, own = 1.0, jax.random.fold_in(stream_key, 6)
    for axis_at, blocks in pieces:
        draws = jnp.exp(jax.random.uniform(jax.random.fold_in(own, axis_at), (blocks,), jnp.float32, smallest / len(pieces), top_value / len(pieces)))
        gain = gain * jnp.repeat(draws, dims[axis_at] // blocks).reshape([-1 if axis == axis_at else 1 for axis in range(len(dims))])
    return gain


def centred(own_key, extent, width, bound, cuts=(), kind=jnp.bfloat16):
    entries = jax.random.normal(own_key, extent, jnp.float32) * width
    if len(cuts) > 0:
        entries = levels(own_key, extent, cuts, -0.22, 0.18) * entries
    return jnp.clip(entries, min=-bound, max=bound).astype(kind)


def setup_inputs(seed: int = 0, part: int = 0) -> dict:
    key_of = jax.random.split(jax.random.key(seed), 8)
    own_keys = jax.random.split(jax.random.fold_in(key_of[7], part), 8)
    return {
        "tokens": centred(own_keys[0], (TOKENS, D), 1.0, 6.0, ((0, 4),)),
        "weight": centred(key_of[1], (D, FF), D ** -0.5, 0.09375, ((1, 4),)),
        "grad_act": centred(own_keys[2], (TOKENS, FF), 1.0, 6.0, ((0, 4), (1, 4))),
        "proj_in": centred(key_of[3], (D, K_IN), D ** -0.5, 0.09375, ((0, 4),)),
        "proj_out": centred(key_of[4], (FF, K_OUT), FF ** -0.5, 0.046875, ((0, 4),)),
        "query_bank": centred(own_keys[5], (QBANK, SK), 1.0, 6.0, ((0, 4),), jnp.float32),
        "query_index": draw_query_index(jax.random.fold_in(jax.random.fold_in(key_of[7], part), 71), part),
    }


def reference(tokens, weight, grad_act, proj_in, proj_out, query_bank, query_index):
    preact = jnp.dot(tokens, weight, preferred_element_type=jnp.float32)
    sigmoid_pre = jax.nn.sigmoid(preact)
    slopes = sigmoid_pre * (1.0 + preact * (1.0 - sigmoid_pre))
    grad_pre = (grad_act.astype(jnp.float32) * slopes).astype(jnp.bfloat16)
    summed = lax.dot_general(weight, grad_pre, (((1,), (1,)), ((), ())), preferred_element_type=jnp.float32)
    grad_in_t = summed.astype(jnp.bfloat16)
    factor_in = jnp.dot(tokens, proj_in, preferred_element_type=jnp.float32)
    factor_out = jnp.dot(grad_pre, proj_out, preferred_element_type=jnp.float32)
    docs_in = factor_in.reshape(DOCS, LEN, K_IN)
    docs_out = factor_out.reshape(DOCS, LEN, K_OUT)
    sketches = jnp.einsum('dti,dtj->dij', docs_out, docs_in, precision=lax.Precision.HIGHEST)
    sketches = sketches.reshape(DOCS, SK) / math.sqrt(LEN)
    gram = jnp.dot(sketches.T, sketches, precision=lax.Precision.HIGHEST)
    chosen = jnp.take(query_bank, query_index.astype(jnp.int32), axis=0)
    scores = jnp.dot(sketches, chosen.T, precision=lax.Precision.HIGHEST) / math.sqrt(SK)
    return (grad_in_t, gram, scores)
```

```python
import math

import jax
import jax.numpy as jnp
from jax import lax
from jax.sharding import PartitionSpec as P

LEN = 256
SK = 4096
HIGH = lax.Precision.HIGHEST


def line_pairs(count, step, color):
    up = [(i, i + 1) for i in range(count - 1) if i < step and i % 2 == color]
    down = [(j, j - 1) for j in range(1, count) if count - 1 - j < step and (j - 1) % 2 == color]
    return up + down


def swap_sum(x, axis, count):
    hop = 1
    while hop < count:
        x = x + lax.ppermute(x, axis, [(i, i ^ hop) for i in range(count)])
        hop *= 2
    return x


def swap_gather(x, axis, count, pos, dim):
    hop = 1
    while hop < count:
        other = lax.ppermute(x, axis, [(i, i ^ hop) for i in range(count)])
        low = (pos // hop) % 2 == 0
        x = jnp.where(low, jnp.concatenate([x, other], dim), jnp.concatenate([other, x], dim))
        hop *= 2
    return x


def body(tokens, weight, grad_act, proj_in, proj_out, query_bank, query_index):
    n = lax.axis_size("tensor")
    m = lax.axis_size("dp")
    pos = lax.axis_index("tensor")
    dp_pos = lax.axis_index("dp")
    docs = tokens.shape[0] // LEN
    feat = proj_in.shape[0]
    sign = jnp.where(pos % 2 == 0, -1, 1)

    tok_cols = lax.dynamic_slice_in_dim(tokens, pos * feat, feat, 1)
    factor_in = swap_sum(jnp.dot(tok_cols, proj_in, preferred_element_type=jnp.float32), "tensor", n)

    halves = 2
    chunk = feat // halves
    grads = []
    for d in range(docs):
        rows = slice(d * LEN, (d + 1) * LEN)
        preact = jnp.dot(tokens[rows], weight, preferred_element_type=jnp.float32)
        sig = jax.nn.sigmoid(preact)
        slopes = sig * (1.0 + preact * (1.0 - sig))
        grads.append((grad_act[rows].astype(jnp.float32) * slopes).astype(jnp.bfloat16))

    def block(k, d, r):
        start = ((pos + sign * k) % n) * feat + r * chunk
        part = lax.dynamic_slice_in_dim(weight, start, chunk, 0)
        return lax.dot_general(part, grads[d], (((1,), (1,)), ((), ())), preferred_element_type=jnp.float32)

    outs = [[None] * halves for _ in range(docs)]
    cells = [(d, r) for d in range(docs) for r in range(halves)]
    blocks = {}
    for k in list(range(1, n)) + [0]:
        for d, r in cells:
            blocks[k, d, r] = block(k, d, r)
    even = {c: None for c in cells}
    odd = {c: None for c in cells}
    for step in range(1, n):
        for c in cells:
            send_even = blocks[(step, *c)]
            if odd[c] is not None:
                send_even = send_even + odd[c]
            new_even = lax.ppermute(send_even, "tensor", line_pairs(n, step, 0))
            new_odd = None
            if line_pairs(n, step, 1):
                send_odd = blocks[(n - step, *c)] + even[c]
                new_odd = lax.ppermute(send_odd, "tensor", line_pairs(n, step, 1))
            even[c], odd[c] = new_even, new_odd
    for d, r in cells:
        total = blocks[0, d, r] + even[d, r]
        if odd[d, r] is not None:
            total = total + odd[d, r]
        outs[d][r] = total.astype(jnp.bfloat16)
    grad_in_t = jnp.concatenate([jnp.concatenate(row, 0) for row in outs], 1)

    sketches = []
    for d in range(docs):
        part_out = jnp.dot(grads[d], proj_out, preferred_element_type=jnp.float32)
        sketches.append(
            lax.dot_general(part_out, factor_in[d * LEN:(d + 1) * LEN], (((0,), (0,)), ((), ())), precision=HIGH)
        )
    sketches = jnp.stack(sketches).reshape(docs, SK) / math.sqrt(LEN)
    sketches = swap_sum(sketches, "tensor", n)
    everyone = swap_gather(sketches, "dp", m, dp_pos, 0)
    gram_rows = SK // (m * n)
    mine = lax.dynamic_slice_in_dim(everyone, (dp_pos * n + pos) * gram_rows, gram_rows, 1)
    gram = lax.dot_general(mine, everyone, (((0,), (0,)), ((), ())), precision=HIGH)

    scores = lax.dot_general(everyone, query_bank, (((1,), (1,)), ((), ())), precision=HIGH) / math.sqrt(SK)
    scores = swap_gather(scores, "dp", m, dp_pos, 1)
    scores = lax.dynamic_slice_in_dim(scores, dp_pos * docs, docs, 0)
    places = jnp.arange(scores.shape[1], dtype=query_index.dtype)
    picked = jnp.where(query_index[None, :, None] == places[None, None, :], scores[:, None, :], 0.0)
    return (grad_in_t, gram, jnp.sum(picked, -1))


def solution(mesh):
    in_specs = (
        P(("groups", "dp"), None),
        P(None, "tensor"),
        P(("groups", "dp"), "tensor"),
        P("tensor", None),
        P("tensor", None),
        P(("groups", "dp"), None),
        P("groups"),
    )
    out_specs = (
        P("tensor", ("groups", "dp")),
        P(("groups", "dp", "tensor"), None),
        P(("groups", "dp"), None),
    )
    return jax.shard_map(body, mesh=mesh, in_specs=in_specs, out_specs=out_specs, check_vma=False)
```

```python
import functools
import math

import jax
import jax.numpy as jnp
from jax import lax
from jax.experimental import pallas as pl
from jax.experimental.pallas import tpu as pltpu
from jax.sharding import PartitionSpec as P

LEN = 256
SK = 4096
HIGH = lax.Precision.HIGHEST
VMEM = 60 << 20
BRIEF = pl.CostEstimate(flops=1, bytes_accessed=1, transcendentals=0)


def widest(size, choices):
    return next(c for c in choices if size % c == 0)


def front_kernel(feat, picks, extra, block_ref, tok_ref, w_ref, act_ref, *refs):
    pieces = [(k, own, feat // split, r) for k, own, split in picks for r in range(split)]
    grad_ref, part_refs = refs[-1 - len(pieces)], refs[len(refs) - len(pieces):]

    @pl.when(pl.program_id(0) == 0)
    def _():
        for part_ref in part_refs:
            part_ref[...] = jnp.zeros_like(part_ref)
        if extra:
            cols_ref, proj_ref = refs[:2]
            factor = lax.dot_general(
                proj_ref[...], cols_ref[...], (((1,), (1,)), ((), ())), preferred_element_type=jnp.float32
            )
            for d in range(factor.shape[1] // LEN):
                at = slice(d * factor.shape[0], (d + 1) * factor.shape[0])
                part_refs[-1][at, :] = factor[:, d * LEN:(d + 1) * LEN]

    preact = jnp.dot(tok_ref[...], w_ref[...], preferred_element_type=jnp.float32)
    sig = 1.0 / (1.0 + jnp.exp(-preact))
    slopes = sig * (1.0 + preact * (1.0 - sig))
    grad = (act_ref[...].astype(jnp.float32) * slopes).astype(jnp.bfloat16).T
    grad_ref[...] = grad
    for part_ref, (k, own, rows, r) in zip(part_refs, pieces):
        start = pl.multiple_of(block_ref[k] * feat + r * rows, rows)
        right = grad if own else refs[0][...]
        part_ref[part_ref.shape[0] - rows:, :] += jnp.dot(w_ref[pl.ds(start, rows), :], right, preferred_element_type=jnp.float32)


def front(doc, blocks, picks, tokens, weight, grad_act, other, proj_in, feat, earlier):
    width, hidden = weight.shape
    cols = widest(hidden, (512, 256, 128))
    rows = [feat // split for _, _, split in picks for _ in range(split)]
    more, more_specs = list(other), [pl.BlockSpec((cols, LEN), lambda j, b: (j, 0))] * len(other)
    if proj_in is not None:
        more = [tokens, proj_in]
        more_specs = [
            pl.BlockSpec((tokens.shape[0], feat), lambda j, b: (0, b[len(picks)])),
            pl.BlockSpec(proj_in.shape, lambda j, b: (0, 0)),
        ]
        rows[-1] += tokens.shape[0] // LEN * proj_in.shape[0]
    return pl.pallas_call(
        functools.partial(front_kernel, feat, picks, proj_in is not None),
        grid_spec=pltpu.PrefetchScalarGridSpec(
            num_scalar_prefetch=1,
            grid=(hidden // cols,),
            in_specs=[
                pl.BlockSpec((LEN, width), lambda j, b: (doc, 0)),
                pl.BlockSpec((width, cols), lambda j, b: (0, j)),
                pl.BlockSpec((LEN, cols), lambda j, b: (doc, j)),
            ]
            + more_specs
            + [pl.BlockSpec(memory_space=pl.ANY)] * len(earlier),
            out_specs=[pl.BlockSpec((cols, LEN), lambda j, b: (j, 0))]
            + [pl.BlockSpec((size, LEN), lambda j, b: (0, 0)) for size in rows],
        ),
        out_shape=[jax.ShapeDtypeStruct((hidden, LEN), jnp.bfloat16)]
        + [jax.ShapeDtypeStruct((size, LEN), jnp.float32) for size in rows],
        compiler_params=pltpu.CompilerParams(vmem_limit_bytes=VMEM),
        cost_estimate=BRIEF,
    )(blocks, tokens, weight, grad_act, *more, *earlier)


def sketch_kernel(widths, proj_ref, in_ref, *refs):
    grads, out_ref = refs[: len(widths)], refs[-1]
    parts = [jnp.dot(proj_ref[...], grad[...], preferred_element_type=jnp.float32) for grad in grads]
    factor_out = jnp.concatenate(parts, 1)
    size = out_ref.shape[2]
    for d in range(out_ref.shape[0]):
        out_ref[d] = lax.dot_general(
            factor_out[:, d * LEN:(d + 1) * LEN],
            in_ref[d * size:(d + 1) * size, :],
            (((1,), (1,)), ((), ())),
            precision=HIGH,
            preferred_element_type=jnp.float32,
        ) / math.sqrt(LEN)


def sketch(proj_out, factor_in, grads, earlier):
    widths = tuple(grad.shape[1] for grad in grads)
    docs = sum(widths) // LEN
    return pl.pallas_call(
        functools.partial(sketch_kernel, widths),
        in_specs=[pl.BlockSpec(memory_space=pltpu.VMEM)] * (2 + len(grads))
        + [pl.BlockSpec(memory_space=pl.ANY)] * len(earlier),
        out_specs=pl.BlockSpec(memory_space=pltpu.VMEM),
        out_shape=jax.ShapeDtypeStruct((docs, proj_out.shape[0], factor_in.shape[0] // docs), jnp.float32),
        compiler_params=pltpu.CompilerParams(vmem_limit_bytes=VMEM),
        cost_estimate=BRIEF,
    )(proj_out, factor_in, *grads, *earlier)


def line_pairs(count, step, color):
    up = [(i, i + 1) for i in range(count - 1) if i < step and i % 2 == color]
    down = [(j, j - 1) for j in range(1, count) if count - 1 - j < step and (j - 1) % 2 == color]
    return up + down


class Total:
    def __init__(self, own, count, hops=()):
        self.own, self.count, self.hops = own, count, list(hops)

    def hop(self):
        step = len(self.hops) + 1
        send = self.own + self.hops[-1] if self.hops else self.own
        pairs = [(step - 1, step), (self.count - step, self.count - step - 1)]
        self.hops.append(lax.ppermute(send, "tensor", pairs))
        return self.hops[-1]

    def result(self):
        return functools.reduce(jnp.add, self.hops, self.own)


def gram_kernel(mine_ref, all_ref, *refs):
    refs[-1][...] = lax.dot_general(
        mine_ref[...], all_ref[...], (((0,), (0,)), ((), ())), precision=HIGH, preferred_element_type=jnp.float32
    )


def gram_rows_of(mine, everyone, earlier):
    docs, rows = mine.shape
    width = everyone.shape[1]
    cols = min(1024, width)
    return pl.pallas_call(
        gram_kernel,
        grid=(width // cols,),
        in_specs=[pl.BlockSpec((docs, rows), lambda j: (0, 0)), pl.BlockSpec((docs, cols), lambda j: (0, j))]
        + [pl.BlockSpec(memory_space=pl.ANY)] * len(earlier),
        out_specs=pl.BlockSpec((rows, cols), lambda j: (0, j)),
        out_shape=jax.ShapeDtypeStruct((rows, width), jnp.float32),
        compiler_params=pltpu.CompilerParams(vmem_limit_bytes=VMEM),
        cost_estimate=BRIEF,
    )(mine, everyone, *earlier)


def after(x, *others):
    return lax.optimization_barrier((x, *others))[0]


SPLITS = (1, 1)


class Line:
    def __init__(self, count):
        self.count = count
        self.blocks = {}
        self.received = {}
        self.sums = {}

    def sum_of(self, step, color, doc, r):
        place = (step, color, doc, r)
        if place not in self.sums:
            block = self.blocks[step if color == 0 else self.count - step, doc, r]
            before = self.send(step - 1, 1 - color, doc, r)
            self.sums[place] = block + before[0] if before else block
        return self.sums[place]

    def send(self, step, color, doc, r):
        place = (step, color, doc, r)
        if place not in self.received and line_pairs(self.count, step, color):
            block = self.sum_of(*place)
            self.received[place] = lax.ppermute(block, "tensor", line_pairs(self.count, step, color))
        return [self.received[place]] if place in self.received else []


def body(tokens, weight, grad_act, proj_in, proj_out, query_bank, query_index):
    n = lax.axis_size("tensor")
    m = lax.axis_size("dp")
    pos = lax.axis_index("tensor")
    dp_pos = lax.axis_index("dp")
    docs = tokens.shape[0] // LEN
    feat = proj_in.shape[0]
    sign = jnp.where(pos % 2 == 0, -1, 1)
    line = Line(n)
    order = (pos + sign * jnp.arange(n, dtype=jnp.int32)) % n

    def make(doc, blocks, picks, other, proj):
        return front(doc, blocks, picks, tokens, weight, grad_act, other, proj, feat, [])

    short = n == 4
    inner = (pos > 0) & (pos < n - 1) & short
    held = (pos + sign * (jnp.arange(2, dtype=jnp.int32) + 1 + jnp.where(inner, jnp.array([1, -1], jnp.int32), 0))) % n
    held = jnp.concatenate([held, pos.astype(jnp.int32).reshape(1)])
    grad, near, far = make(0, held, [(0, True, 1), (1, True, 1)], [], proj_in.T)
    size = far.shape[0] - feat
    near_in, far_in = (lax.ppermute(x, "tensor", line_pairs(n, 1, 0)) for x in (near, far))
    for k, block, arrived in ((1, near, near_in), (2, far[size:], far_in[size:])):
        line.blocks[k, 0, 0], line.received[k, 0, 0, 0] = block, arrived
    picks = [(k % n, True, 1) for k in range(1, n + 1)] + [(k % n, False, 1) for k in range(3, n + 1)]
    other, *parts = make(1, order, picks, [grad], None)
    for (k, own, _), part in zip(picks, parts):
        line.blocks[k, 1 if own else 0, 0] = part
    grads = [grad, other]
    factor_in = Total(far[:size], n, [far_in[:size]])
    if short:
        line.received[2, 1, 0, 0] = lax.ppermute(near + after(near_in, other), "tensor", line_pairs(n, 2, 1))
        far_sum = far + after(far_in, other)
        passed = lax.ppermute(far_sum, "tensor", line_pairs(n, 3, 1))
        line.received[3, 1, 0, 0] = passed[size:]
        factor_in.hops.append(passed[:size])
        line.received[1, 0, 1, 0] = after(line.send(1, 0, 1, 0)[0], far_sum)
        line.received[2, 0, 1, 0] = after(line.send(2, 0, 1, 0)[0], line.sum_of(3, 0, 0, 0))
    while len(factor_in.hops) + 1 < n:
        factor_in.hop()

    def gate(x, *places):
        return after(x, *(line.send(*place)[0] for place in places)) if short else x

    sketches = sketch(proj_out.T, factor_in.result(), grads, []).reshape(docs, SK)
    others = [lax.ppermute(sketches, "tensor", [(i, i ^ far) for i in range(n)]) for far in range(1, n)]
    own = gate(functools.reduce(jnp.add, others, sketches), (3, 0, 0, 0))
    if short:
        own = after(own, line.sum_of(3, 1, 1, 0), line.sum_of(3, 0, 1, 0))
    others = [lax.ppermute(own, "dp", [(i, i ^ far) for i in range(m)]) for far in range(1, m)]
    everyone = jnp.concatenate([own, *others], 0)
    gram_rows = SK // (m * n)
    mine = lax.dynamic_slice_in_dim(everyone, (dp_pos * n + pos) * gram_rows, gram_rows, 1)
    gram = gram_rows_of(mine, everyone, [])
    scores = lax.dot_general(everyone, query_bank, (((1,), (1,)), ((), ())), precision=HIGH) / math.sqrt(SK)
    scores = after(scores, gram)
    parts = [scores[:docs]]
    for far in range(1, m):
        parts.append(lax.ppermute(scores[far * docs:(far + 1) * docs], "dp", [(i, i ^ far) for i in range(m)]))
    scores = jnp.concatenate(parts, 1)
    bank = query_bank.shape[0]
    places = jnp.concatenate([(dp_pos ^ far) * bank + jnp.arange(bank, dtype=query_index.dtype) for far in range(m)])
    for step in range(1, n):
        for doc in range(docs):
            for r in range(SPLITS[doc]):
                line.send(step, 0, doc, r)
                line.send(step, 1, doc, r)

    outs = [[] for _ in range(docs)]
    for doc in range(docs):
        for r in range(SPLITS[doc]):
            total = line.blocks[0, doc, r]
            last = [line.received[n - 1, color, doc, r] for color in (1, 0) if (n - 1, color, doc, r) in line.received]
            for part in lax.optimization_barrier((*last, scores))[:-1] if short and doc == docs - 1 else last:
                total = total + part
            outs[doc].append(total.astype(jnp.bfloat16))
    grad_in_t = jnp.concatenate([jnp.concatenate(row, 0) for row in outs], 1)

    picked = jnp.where(query_index[None, :, None] == places[None, None, :], scores[:, None, :], 0.0)
    return (grad_in_t, gram, jnp.sum(picked, -1))


def solution(mesh):
    in_specs = (
        P(("groups", "dp"), None),
        P(None, "tensor"),
        P(("groups", "dp"), "tensor"),
        P("tensor", None),
        P("tensor", None),
        P(("groups", "dp"), None),
        P("groups"),
    )
    out_specs = (
        P("tensor", ("groups", "dp")),
        P(("groups", "dp", "tensor"), None),
        P(("groups", "dp"), None),
    )
    return jax.shard_map(body, mesh=mesh, in_specs=in_specs, out_specs=out_specs, check_vma=False)
```

```python
import functools
import math

import jax
import jax.numpy as jnp
from jax import lax
from jax.experimental import pallas as pl
from jax.experimental.pallas import tpu as pltpu
from jax.sharding import PartitionSpec as P

LEN = 256
SK = 4096
HIGH = lax.Precision.HIGHEST
VMEM = 60 << 20
BRIEF = pl.CostEstimate(flops=1, bytes_accessed=1, transcendentals=0)


def widest(size, choices):
    return next(c for c in choices if size % c == 0)


def activation_gradient(preact, act):
    sig = 1.0 / (1.0 + jnp.exp(-preact))
    slopes = sig * (1.0 + preact * (1.0 - sig))
    return (act.astype(jnp.float32) * slopes).astype(jnp.bfloat16)


def front_kernel(doc, ahead, picks, lead, n, tok_any, w_any, act_any, extra_any, proj_any, grad_any, *refs):
    part_refs = refs[:len(picks)]
    tok, w, act, grad, pre, extra, proj, single, w_sem, out_sem = refs[len(picks):]
    slices, width, cols = w.shape
    feat = part_refs[-1].shape[0]
    pos = lax.axis_index("tensor")
    rows = pl.ds(doc * LEN, LEN)

    def first_row(k):
        if lead and n == 4:
            k = jnp.where((pos > 0) & (pos < n - 1), 3 - k, k)
        return pl.multiple_of(lax.rem(pos + jnp.where(lax.rem(pos, 2) == 0, n - k, k), n) * feat, feat)
    tok_copy = pltpu.make_async_copy(tok_any.at[rows, :], tok, single.at[0])
    act_copy = pltpu.make_async_copy(act_any.at[rows, :], act, single.at[1])
    if lead:
        place = pl.multiple_of(pos * feat, feat)
        extra_copy = pltpu.make_async_copy(extra_any.at[:, pl.ds(place, feat)], extra, single.at[2])
        proj_copy = pltpu.make_async_copy(proj_any, proj, single.at[3])
    else:
        extra_copy = pltpu.make_async_copy(extra_any, extra, single.at[2])

    def w_copy(j):
        return pltpu.make_async_copy(w_any.at[:, pl.ds(j * cols, cols)], w.at[j], w_sem.at[j])

    def out_copy(j):
        return pltpu.make_async_copy(grad.at[j], grad_any.at[pl.ds(j * cols, cols), :], out_sem.at[j])

    def preact(j):
        w_copy(j).wait()
        return jnp.dot(tok[...], w[j], preferred_element_type=jnp.float32)

    def use(j):
        at = pl.multiple_of(j * cols, cols)
        here = activation_gradient(pre[j % 2], act[:, pl.ds(at, cols)]).T
        grad[j] = here
        for out_ref, (k, own) in zip(part_refs, picks):
            right = here if own else extra[pl.ds(at, cols), :]
            out_ref[out_ref.shape[0] - feat:, :] += jnp.dot(
                w[j, pl.ds(first_row(k), feat), :], right, preferred_element_type=jnp.float32
            )
        out_copy(j).start()

    tok_copy.start()
    w_copy(0).start()
    act_copy.start()
    for j in range(1, ahead):
        w_copy(j).start()
    if not lead:
        extra_copy.start()
    for out_ref in part_refs:
        out_ref[...] = jnp.zeros_like(out_ref)
    tok_copy.wait()
    pre[0] = preact(0)
    act_copy.wait()
    if not lead:
        extra_copy.wait()

    def step(j, carry):
        @pl.when(j + ahead - 1 < slices)
        def _():
            w_copy(j + ahead - 1).start()

        if lead:
            @pl.when(j + ahead - 1 == slices)
            def _():
                extra_copy.start()
                proj_copy.start()

        now = preact(j)
        use(j - 1)
        pre[j % 2] = now
        return carry

    lax.fori_loop(1, slices, step, 0)
    if lead:
        extra_copy.wait()
        proj_copy.wait()
        factor = lax.dot_general(proj[...], extra[...], (((1,), (1,)), ((), ())), preferred_element_type=jnp.float32)
        for d in range(factor.shape[1] // LEN):
            part_refs[0][d * factor.shape[0]:(d + 1) * factor.shape[0], :] = factor[:, d * LEN:(d + 1) * LEN]
    use(slices - 1)
    for j in range(slices):
        out_copy(j).wait()


def front(doc, n, picks, tokens, weight, grad_act, other, proj_in, feat):
    width, hidden = weight.shape
    cols = widest(hidden, (512, 256, 128))
    slices = hidden // cols
    rows = [feat] * len(picks)
    lead = other is None
    if lead:
        rows[0] += tokens.shape[0] // LEN * proj_in.shape[0]
    return pl.pallas_call(
        functools.partial(front_kernel, doc, 3, picks, lead, n),
        grid_spec=pltpu.PrefetchScalarGridSpec(
            num_scalar_prefetch=0,
            grid=(1,),
            in_specs=[pl.BlockSpec(memory_space=pl.ANY)] * 5,
            out_specs=[pl.BlockSpec(memory_space=pl.ANY)] + [pl.BlockSpec((size, LEN), lambda i: (0, 0)) for size in rows],
            scratch_shapes=[
                pltpu.VMEM((LEN, width), jnp.bfloat16),
                pltpu.VMEM((slices, width, cols), jnp.bfloat16),
                pltpu.VMEM((LEN, hidden), jnp.bfloat16),
                pltpu.VMEM((slices, cols, LEN), jnp.bfloat16),
                pltpu.VMEM((2, LEN, cols), jnp.float32),
                pltpu.VMEM((tokens.shape[0], feat) if lead else (hidden, LEN), jnp.bfloat16),
                pltpu.VMEM(proj_in.shape, jnp.bfloat16),
                pltpu.SemaphoreType.DMA((4,)),
                pltpu.SemaphoreType.DMA((slices,)),
                pltpu.SemaphoreType.DMA((slices,)),
            ],
        ),
        out_shape=[jax.ShapeDtypeStruct((hidden, LEN), jnp.bfloat16)]
        + [jax.ShapeDtypeStruct((size, LEN), jnp.float32) for size in rows],
        compiler_params=pltpu.CompilerParams(vmem_limit_bytes=VMEM),
        cost_estimate=BRIEF,
    )(tokens, weight, grad_act, tokens if lead else other, proj_in)


def own_blocks_kernel(block_ref, w_ref, *refs):
    count = len(refs) // 2
    for grad_ref, out_ref in zip(refs[:count], refs[count:]):
        out_ref[...] = jnp.dot(w_ref[...], grad_ref[...], preferred_element_type=jnp.float32)


def own_blocks(blocks, weight, grads, feat):
    hidden = weight.shape[1]
    tile = min(256, feat)
    steps = feat // tile
    return pl.pallas_call(
        own_blocks_kernel,
        grid_spec=pltpu.PrefetchScalarGridSpec(
            num_scalar_prefetch=1,
            grid=(steps,),
            in_specs=[pl.BlockSpec((tile, hidden), lambda i, b: (b[0] * steps + i, 0))]
            + [pl.BlockSpec((hidden, LEN), lambda i, b: (0, 0))] * len(grads),
            out_specs=[pl.BlockSpec((tile, LEN), lambda i, b: (i, 0))] * len(grads),
        ),
        out_shape=[jax.ShapeDtypeStruct((feat, LEN), jnp.float32)] * len(grads),
        compiler_params=pltpu.CompilerParams(vmem_limit_bytes=VMEM),
        cost_estimate=BRIEF,
    )(blocks, weight, *grads)


def sketch_kernel(widths, proj_ref, in_ref, *refs):
    grads, out_ref = refs[: len(widths)], refs[-1]
    parts = [jnp.dot(proj_ref[...], grad[...], preferred_element_type=jnp.float32) for grad in grads]
    factor_out = jnp.concatenate(parts, 1)
    size = out_ref.shape[2]
    for d in range(out_ref.shape[0]):
        out_ref[d] = lax.dot_general(
            factor_out[:, d * LEN:(d + 1) * LEN],
            in_ref[d * size:(d + 1) * size, :],
            (((1,), (1,)), ((), ())),
            precision=HIGH,
            preferred_element_type=jnp.float32,
        ) / math.sqrt(LEN)


def sketch(proj_out, factor_in, grads, earlier):
    widths = tuple(grad.shape[1] for grad in grads)
    docs = sum(widths) // LEN
    return pl.pallas_call(
        functools.partial(sketch_kernel, widths),
        in_specs=[pl.BlockSpec(memory_space=pltpu.VMEM)] * (2 + len(grads))
        + [pl.BlockSpec(memory_space=pl.ANY)] * len(earlier),
        out_specs=pl.BlockSpec(memory_space=pltpu.VMEM),
        out_shape=jax.ShapeDtypeStruct((docs, proj_out.shape[0], factor_in.shape[0] // docs), jnp.float32),
        compiler_params=pltpu.CompilerParams(vmem_limit_bytes=VMEM),
        cost_estimate=BRIEF,
    )(proj_out, factor_in, *grads, *earlier)


def line_pairs(count, step, color):
    up = [(i, i + 1) for i in range(count - 1) if i < step and i % 2 == color]
    down = [(j, j - 1) for j in range(1, count) if count - 1 - j < step and (j - 1) % 2 == color]
    return up + down


class Total:
    def __init__(self, own, count, hops=()):
        self.own, self.count, self.hops = own, count, list(hops)

    def hop(self):
        step = len(self.hops) + 1
        send = self.own + self.hops[-1] if self.hops else self.own
        pairs = [(step - 1, step), (self.count - step, self.count - step - 1)]
        self.hops.append(lax.ppermute(send, "tensor", pairs))
        return self.hops[-1]

    def result(self):
        return functools.reduce(jnp.add, self.hops, self.own)


def gram_kernel(mine_ref, all_ref, *refs):
    refs[-1][...] = lax.dot_general(
        mine_ref[...], all_ref[...], (((0,), (0,)), ((), ())), precision=HIGH, preferred_element_type=jnp.float32
    )


def gram_rows_of(mine, everyone, earlier):
    docs, rows = mine.shape
    width = everyone.shape[1]
    cols = min(1024, width)
    return pl.pallas_call(
        gram_kernel,
        grid=(width // cols,),
        in_specs=[pl.BlockSpec((docs, rows), lambda j: (0, 0)), pl.BlockSpec((docs, cols), lambda j: (0, j))]
        + [pl.BlockSpec(memory_space=pl.ANY)] * len(earlier),
        out_specs=pl.BlockSpec((rows, cols), lambda j: (0, j)),
        out_shape=jax.ShapeDtypeStruct((rows, width), jnp.float32),
        compiler_params=pltpu.CompilerParams(vmem_limit_bytes=VMEM),
        cost_estimate=BRIEF,
    )(mine, everyone, *earlier)


def finish_kernel(done_ref, *refs):
    out_ref, width = refs[-1], done_ref.shape[1]
    out_ref[:, :width] = done_ref[...]
    out_ref[:, width:] = functools.reduce(jnp.add, [ref[...] for ref in refs[:-1]]).astype(out_ref.dtype)


def finish(done, parts):
    feat, width = done.shape
    tile = min(256, feat)
    return pl.pallas_call(
        finish_kernel,
        grid=(feat // tile,),
        in_specs=[pl.BlockSpec((tile, x.shape[1]), lambda i: (i, 0)) for x in (done, *parts)],
        out_specs=pl.BlockSpec((tile, width + parts[0].shape[1]), lambda i: (i, 0)),
        out_shape=jax.ShapeDtypeStruct((feat, width + parts[0].shape[1]), done.dtype),
        compiler_params=pltpu.CompilerParams(vmem_limit_bytes=16 << 20),
        cost_estimate=BRIEF,
    )(done, *parts)


def after(x, *others):
    return lax.optimization_barrier((x, *others))[0]


class Line:
    def __init__(self, count):
        self.count = count
        self.blocks = {}
        self.received = {}
        self.sums = {}

    def sum_of(self, step, color, doc, r):
        place = (step, color, doc, r)
        if place not in self.sums:
            block = self.blocks[step if color == 0 else self.count - step, doc, r]
            before = self.send(step - 1, 1 - color, doc, r)
            self.sums[place] = block + before[0] if before else block
        return self.sums[place]

    def send(self, step, color, doc, r):
        place = (step, color, doc, r)
        if place not in self.received and line_pairs(self.count, step, color):
            block = self.sum_of(*place)
            self.received[place] = lax.ppermute(block, "tensor", line_pairs(self.count, step, color))
        return [self.received[place]] if place in self.received else []


def body(tokens, weight, grad_act, proj_in, proj_out, query_bank, query_index):
    n = lax.axis_size("tensor")
    m = lax.axis_size("dp")
    pos = lax.axis_index("tensor")
    dp_pos = lax.axis_index("dp")
    docs = tokens.shape[0] // LEN
    feat = proj_in.shape[0]
    sign = jnp.where(pos % 2 == 0, -1, 1)
    line = Line(n)
    order = (pos + sign * jnp.arange(n, dtype=jnp.int32)) % n

    short = n == 4
    grad, near, far = front(0, n, [(1, True), (2, True)], tokens, weight, grad_act, None, proj_in.T, feat)
    size = near.shape[0] - feat
    near_in, far_in = (lax.ppermute(x, "tensor", line_pairs(n, 1, 0)) for x in (near, far))
    for k, block, arrived in ((1, near[size:], near_in[size:]), (2, far, far_in)):
        line.blocks[k, 0, 0], line.received[k, 0, 0, 0] = block, arrived
    picks = [(k, True) for k in range(1, n)] + [(k, False) for k in range(3, n)]
    other, *parts = front(1, n, picks, tokens, weight, grad_act, grad, proj_in.T, feat)
    for (k, own), part in zip(picks, parts):
        line.blocks[k, 1 if own else 0, 0] = part
    grads = [grad, other]
    factor_in = Total(near[:size], n, [after(near_in, other, far_in)[:size]])
    if short:
        near_sum = near[size:] + after(near_in, other)[size:]
        line.received[2, 1, 0, 0] = lax.ppermute(near_sum, "tensor", line_pairs(n, 2, 1))
        factor_in.hop()
        factor_in.hops[-1] = after(factor_in.hops[-1], line.received[2, 1, 0, 0])
    while len(factor_in.hops) + 1 < n:
        factor_in.hop()

    def gate(x, *places):
        return after(x, *(line.send(*place)[0] for place in places)) if short else x

    sketches = sketch(proj_out.T, factor_in.result(), grads, []).reshape(docs, SK)
    if short:
        line.received[1, 0, 1, 0] = after(line.send(1, 0, 1, 0)[0], sketches)
        far_sum = far + after(far_in, line.sum_of(2, 1, 1, 0))
        line.received[3, 1, 0, 0] = lax.ppermute(far_sum, "tensor", line_pairs(n, 3, 1))
        line.received[2, 0, 1, 0] = after(line.send(2, 0, 1, 0)[0], line.sum_of(3, 0, 0, 0))
    others = [lax.ppermute(sketches, "tensor", [(i, i ^ far) for i in range(n)]) for far in range(1, n)]
    own = functools.reduce(jnp.add, others, sketches)
    if short:
        own = after(own, line.sum_of(3, 0, 1, 0), line.sum_of(3, 1, 1, 0))
    others = [lax.ppermute(own, "dp", [(i, i ^ far) for i in range(m)]) for far in range(1, m)]
    line.blocks[0, 0, 0], line.blocks[0, 1, 0] = own_blocks(order, weight, [after(grad, own), other], feat)
    everyone = gate(after(jnp.concatenate([own, *others], 0), line.blocks[0, 1, 0]), (3, 0, 0, 0), (3, 1, 0, 0))
    gram_rows = SK // (m * n)
    mine = lax.dynamic_slice_in_dim(everyone, (dp_pos * n + pos) * gram_rows, gram_rows, 1)
    gram = gram_rows_of(mine, everyone, [])
    scores = lax.dot_general(everyone, query_bank, (((1,), (1,)), ((), ())), precision=HIGH) / math.sqrt(SK)
    scores = after(scores, gram)
    parts = [scores[:docs]]
    for far in range(1, m):
        parts.append(lax.ppermute(scores[far * docs:(far + 1) * docs], "dp", [(i, i ^ far) for i in range(m)]))
    scores = jnp.concatenate(parts, 1)
    bank = query_bank.shape[0]
    places = jnp.concatenate([(dp_pos ^ far) * bank + jnp.arange(bank, dtype=query_index.dtype) for far in range(m)])
    for step in range(1, n):
        for doc in range(docs):
            for r in range(1):
                line.send(step, 0, doc, r)
                line.send(step, 1, doc, r)

    ends = []
    for doc in range(docs):
        last = [line.received[n - 1, color, doc, 0] for color in (1, 0) if (n - 1, color, doc, 0) in line.received]
        if short and doc == docs - 1:
            last = lax.optimization_barrier((*last, scores))[:-1]
        ends.append([line.blocks[0, doc, 0], *last])
    grad_in_t = finish(functools.reduce(jnp.add, ends[0]).astype(jnp.bfloat16), ends[1])

    picked = jnp.where(query_index[None, :, None] == places[None, None, :], scores[:, None, :], 0.0)
    return (grad_in_t, gram, jnp.sum(picked, -1))


def solution(mesh):
    in_specs = (
        P(("groups", "dp"), None),
        P(None, "tensor"),
        P(("groups", "dp"), "tensor"),
        P("tensor", None),
        P("tensor", None),
        P(("groups", "dp"), None),
        P("groups"),
    )
    out_specs = (
        P("tensor", ("groups", "dp")),
        P(("groups", "dp", "tensor"), None),
        P(("groups", "dp"), None),
    )
    return jax.shard_map(body, mesh=mesh, in_specs=in_specs, out_specs=out_specs, check_vma=False)
```

```python
import functools
import math

import jax
import jax.numpy as jnp
from jax import lax
from jax.experimental import pallas as pl
from jax.experimental.pallas import tpu as pltpu
from jax.sharding import PartitionSpec as P

LEN = 256
SK = 4096
HIGH = lax.Precision.HIGHEST
VMEM = 60 << 20
BRIEF = pl.CostEstimate(flops=1, bytes_accessed=1, transcendentals=0)


def widest(size, choices):
    return next(c for c in choices if size % c == 0)


def activation_gradient(preact, act):
    sig = 1.0 / (1.0 + jnp.exp(-preact))
    slopes = sig * (1.0 + preact * (1.0 - sig))
    return (act.astype(jnp.float32) * slopes).astype(jnp.bfloat16)


def front_kernel(doc, ahead, picks, lead, n, tok_any, w_any, act_any, extra_any, proj_any, grad_any, *refs):
    part_refs = refs[:len(picks)]
    tok, w, act, grad, pre, extra, proj, single, w_sem, out_sem = refs[len(picks):]
    slices, width, cols = w.shape
    feat = part_refs[-1].shape[0]
    pos = lax.axis_index("tensor")
    rows = pl.ds(doc * LEN, LEN)

    def first_row(k):
        if lead and n == 4:
            k = jnp.where((pos > 0) & (pos < n - 1), 3 - k, k)
        return pl.multiple_of(lax.rem(pos + jnp.where(lax.rem(pos, 2) == 0, n - k, k), n) * feat, feat)
    tok_copy = pltpu.make_async_copy(tok_any.at[rows, :], tok, single.at[0])
    act_copy = pltpu.make_async_copy(act_any.at[rows, :], act, single.at[1])
    if lead:
        place = pl.multiple_of(pos * feat, feat)
        extra_copy = pltpu.make_async_copy(extra_any.at[:, pl.ds(place, feat)], extra, single.at[2])
        proj_copy = pltpu.make_async_copy(proj_any, proj, single.at[3])
    else:
        extra_copy = pltpu.make_async_copy(extra_any, extra, single.at[2])

    def w_copy(j):
        return pltpu.make_async_copy(w_any.at[:, pl.ds(j * cols, cols)], w.at[j], w_sem.at[j])

    def out_copy(j):
        return pltpu.make_async_copy(grad.at[j], grad_any.at[pl.ds(j * cols, cols), :], out_sem.at[j])

    def preact(j):
        w_copy(j).wait()
        return jnp.dot(tok[...], w[j], preferred_element_type=jnp.float32)

    def use(j):
        at = pl.multiple_of(j * cols, cols)
        here = activation_gradient(pre[j % 2], act[:, pl.ds(at, cols)]).T
        grad[j] = here
        for out_ref, (k, own) in zip(part_refs, picks):
            right = here if own else extra[pl.ds(at, cols), :]
            out_ref[out_ref.shape[0] - feat:, :] += jnp.dot(
                w[j, pl.ds(first_row(k), feat), :], right, preferred_element_type=jnp.float32
            )
        out_copy(j).start()

    tok_copy.start()
    w_copy(0).start()
    act_copy.start()
    for j in range(1, ahead):
        w_copy(j).start()
    if not lead:
        extra_copy.start()
    for out_ref in part_refs:
        out_ref[...] = jnp.zeros_like(out_ref)
    tok_copy.wait()
    pre[0] = preact(0)
    act_copy.wait()
    if not lead:
        extra_copy.wait()

    def step(j, carry):
        @pl.when(j + ahead - 1 < slices)
        def _():
            w_copy(j + ahead - 1).start()

        if lead:
            @pl.when(j + ahead - 1 == slices)
            def _():
                extra_copy.start()
                proj_copy.start()

        now = preact(j)
        use(j - 1)
        pre[j % 2] = now
        return carry

    lax.fori_loop(1, slices, step, 0)
    if lead:
        extra_copy.wait()
        proj_copy.wait()
        factor = lax.dot_general(proj[...], extra[...], (((1,), (1,)), ((), ())), preferred_element_type=jnp.float32)
        for d in range(factor.shape[1] // LEN):
            part_refs[0][d * factor.shape[0]:(d + 1) * factor.shape[0], :] = factor[:, d * LEN:(d + 1) * LEN]
    use(slices - 1)
    for j in range(slices):
        out_copy(j).wait()


def front(doc, n, picks, tokens, weight, grad_act, other, proj_in, feat):
    width, hidden = weight.shape
    cols = widest(hidden, (512, 256, 128))
    slices = hidden // cols
    rows = [feat] * len(picks)
    lead = other is None
    if lead:
        rows[0] += tokens.shape[0] // LEN * proj_in.shape[0]
    return pl.pallas_call(
        functools.partial(front_kernel, doc, 3, picks, lead, n),
        grid_spec=pltpu.PrefetchScalarGridSpec(
            num_scalar_prefetch=0,
            grid=(1,),
            in_specs=[pl.BlockSpec(memory_space=pl.ANY)] * 5,
            out_specs=[pl.BlockSpec(memory_space=pl.ANY)] + [pl.BlockSpec((size, LEN), lambda i: (0, 0)) for size in rows],
            scratch_shapes=[
                pltpu.VMEM((LEN, width), jnp.bfloat16),
                pltpu.VMEM((slices, width, cols), jnp.bfloat16),
                pltpu.VMEM((LEN, hidden), jnp.bfloat16),
                pltpu.VMEM((slices, cols, LEN), jnp.bfloat16),
                pltpu.VMEM((2, LEN, cols), jnp.float32),
                pltpu.VMEM((tokens.shape[0], feat) if lead else (hidden, LEN), jnp.bfloat16),
                pltpu.VMEM(proj_in.shape, jnp.bfloat16),
                pltpu.SemaphoreType.DMA((4,)),
                pltpu.SemaphoreType.DMA((slices,)),
                pltpu.SemaphoreType.DMA((slices,)),
            ],
        ),
        out_shape=[jax.ShapeDtypeStruct((hidden, LEN), jnp.bfloat16)]
        + [jax.ShapeDtypeStruct((size, LEN), jnp.float32) for size in rows],
        compiler_params=pltpu.CompilerParams(vmem_limit_bytes=VMEM),
        cost_estimate=BRIEF,
    )(tokens, weight, grad_act, tokens if lead else other, proj_in)


def own_blocks_kernel(block_ref, w_ref, *refs):
    count = len(refs) // 2
    for grad_ref, out_ref in zip(refs[:count], refs[count:]):
        out_ref[...] = jnp.dot(w_ref[...], grad_ref[...], preferred_element_type=jnp.float32)


def own_blocks(blocks, weight, grads, feat):
    hidden = weight.shape[1]
    tile = min(256, feat)
    steps = feat // tile
    return pl.pallas_call(
        own_blocks_kernel,
        grid_spec=pltpu.PrefetchScalarGridSpec(
            num_scalar_prefetch=1,
            grid=(steps,),
            in_specs=[pl.BlockSpec((tile, hidden), lambda i, b: (b[0] * steps + i, 0))]
            + [pl.BlockSpec((hidden, LEN), lambda i, b: (0, 0))] * len(grads),
            out_specs=[pl.BlockSpec((tile, LEN), lambda i, b: (i, 0))] * len(grads),
        ),
        out_shape=[jax.ShapeDtypeStruct((feat, LEN), jnp.float32)] * len(grads),
        compiler_params=pltpu.CompilerParams(vmem_limit_bytes=VMEM),
        cost_estimate=BRIEF,
    )(blocks, weight, *grads)


def sketch_kernel(widths, proj_ref, in_ref, *refs):
    grads, out_ref = refs[: len(widths)], refs[-1]
    parts = [jnp.dot(proj_ref[...], grad[...], preferred_element_type=jnp.float32) for grad in grads]
    factor_out = jnp.concatenate(parts, 1)
    size = out_ref.shape[2]
    for d in range(out_ref.shape[0]):
        out_ref[d] = lax.dot_general(
            factor_out[:, d * LEN:(d + 1) * LEN],
            in_ref[d * size:(d + 1) * size, :],
            (((1,), (1,)), ((), ())),
            precision=HIGH,
            preferred_element_type=jnp.float32,
        ) / math.sqrt(LEN)


def sketch(proj_out, factor_in, grads, earlier):
    widths = tuple(grad.shape[1] for grad in grads)
    docs = sum(widths) // LEN
    return pl.pallas_call(
        functools.partial(sketch_kernel, widths),
        in_specs=[pl.BlockSpec(memory_space=pltpu.VMEM)] * (2 + len(grads))
        + [pl.BlockSpec(memory_space=pl.ANY)] * len(earlier),
        out_specs=pl.BlockSpec(memory_space=pltpu.VMEM),
        out_shape=jax.ShapeDtypeStruct((docs, proj_out.shape[0], factor_in.shape[0] // docs), jnp.float32),
        compiler_params=pltpu.CompilerParams(vmem_limit_bytes=VMEM),
        cost_estimate=BRIEF,
    )(proj_out, factor_in, *grads, *earlier)


def line_pairs(count, step, color):
    up = [(i, i + 1) for i in range(count - 1) if i < step and i % 2 == color]
    down = [(j, j - 1) for j in range(1, count) if count - 1 - j < step and (j - 1) % 2 == color]
    return up + down


class Total:
    def __init__(self, own, count, hops=()):
        self.own, self.count, self.hops = own, count, list(hops)

    def hop(self):
        step = len(self.hops) + 1
        send = self.own + self.hops[-1] if self.hops else self.own
        pairs = [(step - 1, step), (self.count - step, self.count - step - 1)]
        self.hops.append(lax.ppermute(send, "tensor", pairs))
        return self.hops[-1]

    def result(self):
        return functools.reduce(jnp.add, self.hops, self.own)


def gram_kernel(mine_ref, all_ref, *refs):
    refs[-1][...] = lax.dot_general(
        mine_ref[...], all_ref[...], (((0,), (0,)), ((), ())), precision=HIGH, preferred_element_type=jnp.float32
    )


def gram_rows_of(mine, everyone, earlier):
    docs, rows = mine.shape
    width = everyone.shape[1]
    cols = min(1024, width)
    return pl.pallas_call(
        gram_kernel,
        grid=(width // cols,),
        in_specs=[pl.BlockSpec((docs, rows), lambda j: (0, 0)), pl.BlockSpec((docs, cols), lambda j: (0, j))]
        + [pl.BlockSpec(memory_space=pl.ANY)] * len(earlier),
        out_specs=pl.BlockSpec((rows, cols), lambda j: (0, j)),
        out_shape=jax.ShapeDtypeStruct((rows, width), jnp.float32),
        compiler_params=pltpu.CompilerParams(vmem_limit_bytes=VMEM),
        cost_estimate=BRIEF,
    )(mine, everyone, *earlier)


def finish_kernel(done_ref, *refs):
    out_ref, width = refs[-1], done_ref.shape[1]
    out_ref[:, :width] = done_ref[...]
    out_ref[:, width:] = functools.reduce(jnp.add, [ref[...] for ref in refs[:-1]]).astype(out_ref.dtype)


def finish(done, parts):
    feat, width = done.shape
    tile = min(256, feat)
    return pl.pallas_call(
        finish_kernel,
        grid=(feat // tile,),
        in_specs=[pl.BlockSpec((tile, x.shape[1]), lambda i: (i, 0)) for x in (done, *parts)],
        out_specs=pl.BlockSpec((tile, width + parts[0].shape[1]), lambda i: (i, 0)),
        out_shape=jax.ShapeDtypeStruct((feat, width + parts[0].shape[1]), done.dtype),
        compiler_params=pltpu.CompilerParams(vmem_limit_bytes=16 << 20),
        cost_estimate=BRIEF,
    )(done, *parts)


def after(x, *others):
    return lax.optimization_barrier((x, *others))[0]


class Line:
    def __init__(self, count):
        self.count = count
        self.blocks = {}
        self.received = {}
        self.sums = {}

    def sum_of(self, step, color, doc, r):
        place = (step, color, doc, r)
        if place not in self.sums:
            block = self.blocks[step if color == 0 else self.count - step, doc, r]
            before = self.send(step - 1, 1 - color, doc, r)
            self.sums[place] = block + before[0] if before else block
        return self.sums[place]

    def send(self, step, color, doc, r):
        place = (step, color, doc, r)
        if place not in self.received and line_pairs(self.count, step, color):
            block = self.sum_of(*place)
            self.received[place] = lax.ppermute(block, "tensor", line_pairs(self.count, step, color))
        return [self.received[place]] if place in self.received else []


def body(tokens, weight, grad_act, proj_in, proj_out, query_bank, query_index):
    n = lax.axis_size("tensor")
    m = lax.axis_size("dp")
    pos = lax.axis_index("tensor")
    dp_pos = lax.axis_index("dp")
    docs = tokens.shape[0] // LEN
    feat = proj_in.shape[0]
    sign = jnp.where(pos % 2 == 0, -1, 1)
    line = Line(n)
    order = (pos + sign * jnp.arange(n, dtype=jnp.int32)) % n

    short = n == 4
    grad, near, far = front(0, n, [(1, True), (2, True)], tokens, weight, grad_act, None, proj_in.T, feat)
    size = near.shape[0] - feat
    near_in, far_in = (lax.ppermute(x, "tensor", line_pairs(n, 1, 0)) for x in (near, far))
    for k, block, arrived in ((1, near[size:], near_in[size:]), (2, far, far_in)):
        line.blocks[k, 0, 0], line.received[k, 0, 0, 0] = block, arrived
    picks = [(k, True) for k in range(1, n)] + [(k, False) for k in range(3, n)]
    other, *parts = front(1, n, picks, tokens, weight, grad_act, grad, proj_in.T, feat)
    for (k, own), part in zip(picks, parts):
        line.blocks[k, 1 if own else 0, 0] = part
    grads = [grad, other]
    factor_in = Total(near[:size], n, [after(near_in, other, far_in)[:size]])
    if short:
        near_sum = near[size:] + after(near_in, other)[size:]
        line.received[2, 1, 0, 0] = lax.ppermute(near_sum, "tensor", line_pairs(n, 2, 1))
        factor_in.hop()
        factor_in.hops[-1] = after(factor_in.hops[-1], line.received[2, 1, 0, 0])
    while len(factor_in.hops) + 1 < n:
        factor_in.hop()

    def gate(x, *places):
        return after(x, *(line.send(*place)[0] for place in places)) if short else x

    sketches = sketch(proj_out.T, factor_in.result(), grads, []).reshape(docs, SK)
    if short:
        line.received[1, 0, 1, 0] = after(line.send(1, 0, 1, 0)[0], sketches)
        far_sum = far + after(far_in, line.sum_of(2, 1, 1, 0))
        line.received[3, 1, 0, 0] = lax.ppermute(far_sum, "tensor", line_pairs(n, 3, 1))
        held = [after(grad, line.sum_of(2, 1, 1, 0)), other]
        line.blocks[0, 0, 0], line.blocks[0, 1, 0] = own_blocks(order, weight, held, feat)
        ready = (line.sum_of(3, 0, 0, 0), line.blocks[0, 1, 0])
        line.received[2, 0, 1, 0] = after(line.send(2, 0, 1, 0)[0], *ready)
    others = [lax.ppermute(sketches, "tensor", [(i, i ^ far) for i in range(n)]) for far in range(1, n)]
    own = functools.reduce(jnp.add, others, sketches)
    if short:
        own = after(own, line.sum_of(3, 0, 1, 0), line.sum_of(3, 1, 1, 0))
    others = [lax.ppermute(own, "dp", [(i, i ^ far) for i in range(m)]) for far in range(1, m)]
    if not short:
        line.blocks[0, 0, 0], line.blocks[0, 1, 0] = own_blocks(order, weight, grads, feat)
    everyone = gate(after(jnp.concatenate([own, *others], 0), line.blocks[0, 1, 0]), (3, 0, 0, 0), (3, 1, 0, 0))
    gram_rows = SK // (m * n)
    mine = lax.dynamic_slice_in_dim(everyone, (dp_pos * n + pos) * gram_rows, gram_rows, 1)
    gram = gram_rows_of(mine, everyone, [])
    scores = lax.dot_general(everyone, query_bank, (((1,), (1,)), ((), ())), precision=HIGH) / math.sqrt(SK)
    scores = after(scores, gram)
    parts = [scores[:docs]]
    for far in range(1, m):
        parts.append(lax.ppermute(scores[far * docs:(far + 1) * docs], "dp", [(i, i ^ far) for i in range(m)]))
    scores = jnp.concatenate(parts, 1)
    bank = query_bank.shape[0]
    places = jnp.concatenate([(dp_pos ^ far) * bank + jnp.arange(bank, dtype=query_index.dtype) for far in range(m)])
    for step in range(1, n):
        for doc in range(docs):
            for r in range(1):
                line.send(step, 0, doc, r)
                line.send(step, 1, doc, r)

    ends = []
    for doc in range(docs):
        last = [line.received[n - 1, color, doc, 0] for color in (1, 0) if (n - 1, color, doc, 0) in line.received]
        if short and doc == docs - 1:
            last = lax.optimization_barrier((*last, scores))[:-1]
        ends.append([line.blocks[0, doc, 0], *last])
    grad_in_t = finish(functools.reduce(jnp.add, ends[0]).astype(jnp.bfloat16), ends[1])

    picked = jnp.where(query_index[None, :, None] == places[None, None, :], scores[:, None, :], 0.0)
    return (grad_in_t, gram, jnp.sum(picked, -1))


def solution(mesh):
    in_specs = (
        P(("groups", "dp"), None),
        P(None, "tensor"),
        P(("groups", "dp"), "tensor"),
        P("tensor", None),
        P("tensor", None),
        P(("groups", "dp"), None),
        P("groups"),
    )
    out_specs = (
        P("tensor", ("groups", "dp")),
        P(("groups", "dp", "tensor"), None),
        P(("groups", "dp"), None),
    )
    return jax.shard_map(body, mesh=mesh, in_specs=in_specs, out_specs=out_specs, check_vma=False)
```
